32 devices in a mesh: band: 4 (over z), mem: 8 (over y, x, core).
Axes of the slice: x: 2, y: 2, z: 4, core: 2. Of those that a mesh axis runs over, the one named last changes fastest.
Arguments:
- prior_ensemble: bfloat16 [1024, 65536], P('mem', 'band'), may hold values from -6 to 6
- perturbed_measurements: bfloat16 [1024, 4096], P('mem', 'band'), may hold values from -6 to 6
- solved_residuals: bfloat16 [1024, 4096], P('mem', 'band'), may hold values from -6 to 6
- localisation_matrix: float32 [8, 128, 128], replicated, may hold values from 0 to 1
- piece_owner_device: int32 [512], P('band'), may hold values from 0 to 7, as said below
- measurement_group_matrix: int32 [512, 6], P('band'), may hold values from 0 to 31, as said below
- localisation_factors: int32 [512, 6], P('band'), may hold values from 0 to 7
Outputs:
- analysis: bfloat16 [1024, 65536], P('mem', 'band')
- spread: float32 [1024, 128], P(('band', 'mem'))
The draws below stay inside these ranges and needn't reach their ends.
Inputs may be any that keep to these rules, and one draw needn't show every extreme that they name: `piece_owner_device`: within a band, no owner has more than 32 patches, and in every band one owner has exactly 32. `measurement_group_matrix`: patch p of band b = p // 128 has the centre block c = b * 8 + (p - b * 128) // 16 and uses only blocks c - 2 to c + 2.
All inputs are finite; a program needn't handle non-finite values.
Results may differ from the reference program's by a relative error of at most 0.0065.
Values may be sent and summed in bfloat16 or wider, within the bound.
No kernel may reach another device: no remote copies, remote signals or barrier semaphores. Data moves between devices by JAX's collectives and lax.ppermute only.
A program may use at most 192 MiB of HBM per device.

```python
import jax
import jax.numpy as jnp
from jax import lax

ENSEMBLE_SIZE = 1024
PIECE_SPAN = 128
OBLK = 128
NBLK = 6
NTAPER = 8
RIM_BLOCKS = 2
PATCH_DEV = 16
CAP = 32
PIECES_PER_STRIP = 128
PATCHES = 512
VECTOR_SPAN = 65536
OB_BAND = 8
NOBS_BLK = 32
NOBS = 4096
SLOTS = 1024
N_BAND = 4
N_MEM = 8


def draw_piece_owner_device(key, part):
    owner_count = PIECES_PER_STRIP // PATCH_DEV

    def one_band(band_key):
        key_heavy, key_pick, key_order = jax.random.split(band_key, 3)
        heavy = jax.random.randint(key_heavy, (), 0, owner_count)
        picked = jax.random.permutation(key_pick, (owner_count - 1) * CAP)[:PIECES_PER_STRIP - CAP]
        others = (picked // CAP).astype(jnp.int32)
        others = others + (others >= heavy).astype(jnp.int32)
        labels = jnp.concatenate([jnp.full((CAP,), heavy, jnp.int32), others])
        shuffle = jax.random.permutation(key_order, PIECES_PER_STRIP)
        return labels[shuffle].astype(jnp.int32)
    band_keys = jax.random.split(jax.random.fold_in(key, 11), PATCHES // PIECES_PER_STRIP)
    return jax.vmap(one_band)(band_keys).reshape(PATCHES)


def draw_measurement_group_matrix(key, part):
    patch = jnp.arange(PATCHES, dtype=jnp.int32)
    strip_position = patch // PIECES_PER_STRIP
    within = patch % PIECES_PER_STRIP
    centre = strip_position * OB_BAND + within * OB_BAND // PIECES_PER_STRIP
    offsets = jax.random.randint(jax.random.fold_in(key, 23), (PATCHES, NBLK), -RIM_BLOCKS, RIM_BLOCKS + 1)
    return jnp.clip(centre[:, None] + offsets, 0, NOBS_BLK - 1).astype(jnp.int32)


def touch_ends(drawn, own_key, smallest, high):
    extent = drawn.shape
    place = [jax.random.randint(jax.random.fold_in(own_key, axis), (), 0, extent[axis]) for axis in range(len(extent))]
    drawn = drawn.at[tuple(place)].set(smallest)
    longest = extent.index(max(extent))
    place[longest] = (place[longest] + 1) % extent[longest]
    return drawn.at[tuple(place)].set(high)


def shard_levels(rng, shape, cuts, least, largest):
    loudness, own = 1.0, jax.random.fold_in(rng, 6)
    for axis_at, blocks in cuts:
        draws = jnp.exp(jax.random.uniform(jax.random.fold_in(own, axis_at), (blocks,), jnp.float32, least / len(cuts), largest / len(cuts)))
        loudness = loudness * jnp.repeat(draws, shape[axis_at] // blocks).reshape([-1 if axis == axis_at else 1 for axis in range(len(shape))])
    return loudness


def bell_draw(key, dims, scale, reach, cuts=(), kind=jnp.bfloat16):
    array = scale * jax.random.normal(key, dims, jnp.float32)
    if cuts:
        array = array * shard_levels(key, dims, cuts, -0.22, 0.18)
    return jnp.clip(array, -reach, reach).astype(kind)


def setup_inputs(seed: int = 0) -> dict:
    seeds = jax.random.split(jax.random.key(seed), 8)
    return {
        "prior_ensemble": bell_draw(seeds[0], (ENSEMBLE_SIZE, VECTOR_SPAN), 1.0, 6.0, ((0, 8), (1, 4))),
        "perturbed_measurements": bell_draw(seeds[1], (ENSEMBLE_SIZE, NOBS), 1.0, 6.0, ((0, 8), (1, 4))),
        "solved_residuals": bell_draw(seeds[2], (ENSEMBLE_SIZE, NOBS), 1.0, 6.0, ((0, 8), (1, 4))),
        "localisation_matrix": jnp.clip(jax.random.uniform(seeds[3], (NTAPER, PIECE_SPAN, OBLK), jnp.float32, 0.0, 1.0), 0.0, 1.0),
        "piece_owner_device": draw_piece_owner_device(jax.random.fold_in(seeds[7], 71), 0),
        "measurement_group_matrix": draw_measurement_group_matrix(jax.random.fold_in(seeds[7], 71), 0),
        "localisation_factors": touch_ends(jax.random.randint(seeds[6], (PATCHES, NBLK), 0, NTAPER), jax.random.fold_in(seeds[6], 1), 0, NTAPER - 1).astype(jnp.int32),
    }


def reference(prior_ensemble, perturbed_measurements, solved_residuals, localisation_matrix, piece_owner_device, measurement_group_matrix, localisation_factors):
    prior_per_strip = prior_ensemble.reshape(ENSEMBLE_SIZE, N_BAND, PIECES_PER_STRIP, PIECE_SPAN)
    obs_float = perturbed_measurements.astype(jnp.float32)
    obs_centre = jnp.mean(obs_float, axis=0)
    obs_dev = (obs_float - obs_centre).astype(jnp.bfloat16).reshape(ENSEMBLE_SIZE, NOBS_BLK, OBLK)
    solved = solved_residuals.reshape(ENSEMBLE_SIZE, NOBS_BLK, OBLK)

    def one_band(strip_position):
        ensemble_vectors = lax.dynamic_index_in_dim(prior_per_strip, strip_position, 1, keepdims=False)
        block_rows = lax.dynamic_slice_in_dim(measurement_group_matrix, strip_position * PIECES_PER_STRIP, PIECES_PER_STRIP, 0)
        taper_rows = lax.dynamic_slice_in_dim(localisation_factors, strip_position * PIECES_PER_STRIP, PIECES_PER_STRIP, 0)
        members_float = ensemble_vectors.astype(jnp.float32)
        centre = jnp.mean(members_float, axis=0)
        state_dev = (members_float - centre).astype(jnp.bfloat16)
        increment = jnp.zeros((ENSEMBLE_SIZE, PIECES_PER_STRIP, PIECE_SPAN), jnp.float32)
        for block_id in range(NBLK):
            obs_piece = jnp.take(obs_dev, block_rows[:, block_id], axis=1)
            solved_piece = jnp.take(solved, block_rows[:, block_id], axis=1)
            covariance = jnp.einsum("mie,mio->ieo", state_dev.astype(jnp.float32), obs_piece.astype(jnp.float32)) / (ENSEMBLE_SIZE - 1)
            weights = jnp.take(localisation_matrix, taper_rows[:, block_id], axis=0)
            tapered = (weights * covariance).astype(jnp.bfloat16)
            increment = increment + jnp.einsum("ieo,mio->mie", tapered.astype(jnp.float32), solved_piece.astype(jnp.float32))
        updated = (members_float + increment).astype(jnp.bfloat16)
        updated_float = updated.astype(jnp.float32)
        upd_centre = jnp.mean(updated_float, axis=0)
        variance = jnp.mean((updated_float - upd_centre) ** 2, axis=0)
        return updated, variance

    updated, variance = lax.map(one_band, jnp.arange(N_BAND))
    analysis = jnp.transpose(updated, (1, 0, 2, 3)).reshape(ENSEMBLE_SIZE, VECTOR_SPAN)
    owners = piece_owner_device.reshape(N_BAND, PIECES_PER_STRIP)
    owner_hits = (owners[:, :, None] == jnp.arange(N_MEM, dtype=jnp.int32)[None, None, :]).astype(jnp.int32)
    before = jnp.cumsum(owner_hits, axis=1) - owner_hits
    slot_rank = jnp.sum(before * owner_hits, axis=2)
    band_base = (jnp.arange(N_BAND, dtype=jnp.int32) * (N_MEM * CAP))[:, None]
    slot_row = (band_base + owners * CAP + slot_rank).astype(jnp.int32)
    spread = jnp.zeros((SLOTS, PIECE_SPAN), jnp.float32).at[slot_row.reshape(-1)].set(variance.reshape(-1, PIECE_SPAN))
    return analysis, spread
```

```python
import functools

import jax
import jax.numpy as jnp
from jax import lax
from jax.experimental import pallas as pl
from jax.experimental.pallas import tpu as pltpu
from jax.sharding import PartitionSpec as P

RIM_BLOCKS = 2
CHUNKS = 2
STEP_PATCHES = 2
PAD_ROWS = 16
VMEM_BYTES = 48 * 1024 * 1024


def prepare_kernel(count, rows, width, obs_len, place_ref, *refs):
    pieces, (ydt_ref, solved_ref, ysum_ref) = refs[:count], refs[count:]
    offset = pl.multiple_of(place_ref[0] * obs_len, obs_len)
    window = pl.ds(offset, width)
    members = count * rows
    total = jnp.zeros((1, width), jnp.float32)
    for piece in pieces:
        total = total + jnp.sum(piece[0, :, window].astype(jnp.float32), axis=0, keepdims=True)
    centre = total / members
    for i, piece in enumerate(pieces):
        place = slice(i * rows, (i + 1) * rows)
        dev = piece[0, :, window].astype(jnp.float32) - centre
        ydt_ref[:width, place] = jnp.transpose(dev).astype(jnp.bfloat16)
        solved_ref[place, :] = piece[1, :, window]
    ydt_ref[width:, :] = jnp.ones((ydt_ref.shape[0] - width, members), jnp.bfloat16)
    ysum_ref[...] = jnp.dot(
        ydt_ref[:width, :],
        jnp.ones((members, ysum_ref.shape[1]), jnp.bfloat16),
        preferred_element_type=jnp.float32,
    )


def analyse_kernel(count, rows, span, obs_len, nblk, block_ref, taper_ref, *refs):
    priors, (ydt_ref, solved_ref, ysum_ref, loc_ref) = refs[:count], refs[count : count + 4]
    outs, (var_ref, weight_ref) = refs[count + 4 : 2 * count + 4], refs[2 * count + 4 :]
    step = pl.program_id(0)
    width = solved_ref.shape[1]
    members = count * rows
    patches = priors[0].shape[1] // span
    weight_ref[...] = jnp.zeros_like(weight_ref)
    for j in range(patches):
        for k in range(nblk):
            at = (step * patches + j) * nblk + k
            row = pl.multiple_of(block_ref[at] * obs_len, obs_len)
            there = (pl.ds(row, obs_len), slice(j * span, (j + 1) * span))
            weight_ref[there] = weight_ref[there] + loc_ref[taper_ref[at]]
    prior = jnp.concatenate([ref[...] for ref in priors], axis=0)
    product = jnp.dot(ydt_ref[...], prior, preferred_element_type=jnp.float32)
    mean = product[width : width + 1, :] * (1.0 / members)
    ysum = jnp.concatenate([ysum_ref[...]] * patches, axis=1)
    cov = product[:width, :] - ysum * mean
    tapered = (cov * weight_ref[...]).astype(jnp.bfloat16)
    increment = jnp.dot(solved_ref[...], tapered, preferred_element_type=jnp.float32)
    updated = (prior.astype(jnp.float32) + increment).astype(jnp.bfloat16)
    for i, out in enumerate(outs):
        out[...] = updated[i * rows : (i + 1) * rows, :]
    updated = updated.astype(jnp.float32)
    centre = jnp.sum(updated, axis=0, keepdims=True) * (1.0 / members)
    variance = jnp.sum((updated - centre) ** 2, axis=0, keepdims=True) * (1.0 / members)
    for j in range(patches):
        var_ref[pl.ds(step * patches + j, 1), :] = variance[:, j * span : (j + 1) * span]


def spread_kernel(per_worker, owner_ref, place_ref, var_ref, out_ref):
    me = place_ref[0]
    out_ref[...] = jnp.zeros_like(out_ref)

    def one(patch, filled):
        mine = owner_ref[patch] == me
        relative = jnp.bitwise_xor(patch // per_worker, me)

        @pl.when(mine)
        def _():
            source = relative * per_worker + patch % per_worker
            out_ref[pl.ds(filled, 1), :] = var_ref[pl.ds(source, 1), :]

        return filled + mine.astype(jnp.int32)

    lax.fori_loop(0, owner_ref.shape[0], one, jnp.int32(0))


def whole(shape):
    return pl.BlockSpec(shape, lambda *_: (0,) * len(shape))


def per_device(
    prior_ensemble,
    perturbed_measurements,
    solved_residuals,
    localisation_matrix,
    piece_owner_device,
    measurement_group_matrix,
    localisation_factors,
):
    rows, vector_span = prior_ensemble.shape
    taper_count, span, obs_len = localisation_matrix.shape
    nblk = measurement_group_matrix.shape[1]
    count, bands = lax.axis_size("mem"), lax.axis_size("band")
    members = rows * count
    strip = vector_span // span
    band_blocks = perturbed_measurements.shape[1] // obs_len
    per_worker = strip // count
    centres = per_worker * band_blocks // strip
    assert centres * strip == per_worker * band_blocks and count & (count - 1) == 0
    window = 2 * RIM_BLOCKS + centres
    width = window * obs_len
    strip_position = lax.axis_index("band")
    me = lax.axis_index("mem")

    def partner(x, flip):
        return lax.ppermute(x, "mem", [(i, i ^ flip) for i in range(count)])

    both = jnp.stack([perturbed_measurements, solved_residuals])
    up = [(i, i + 1) for i in range(bands - 1)]
    down = [(j, i) for i, j in up]
    rim = RIM_BLOCKS * obs_len
    before = lax.ppermute(both[:, :, -rim:], "band", up)
    after = lax.ppermute(both[:, :, :rim], "band", down)
    padded = jnp.concatenate([before, both, after], axis=2)
    pair_width = (window + centres) * obs_len

    def pair_window(flip):
        first = ((me ^ flip) >> 1) * (2 * centres * obs_len)
        return lax.dynamic_slice_in_dim(padded, first, pair_width, 2)

    chunk_patches = per_worker // CHUNKS
    chunk_span = chunk_patches * span

    def outgoing(flip, chunk):
        first = (me ^ flip) * (per_worker * span) + chunk * chunk_span
        return lax.dynamic_slice_in_dim(prior_ensemble, first, chunk_span, 1)

    order = list(range(2, count, 2)) + list(range(3, count, 2)) + [1]

    def scatter_prior(chunk):
        got = {0: outgoing(0, chunk)}
        for flip in order:
            got[flip] = partner(outgoing(flip, chunk), flip)
        return [got[i] for i in range(count)]

    priors = [scatter_prior(0)]
    even = {0: pair_window(0)}
    for flip in range(2, count, 2):
        even[flip] = partner(pair_window(flip), flip)
    pieces = []
    for flip in range(0, count, 2):
        pieces += [even[flip], partner(even[flip], 1)]
    for chunk in range(1, CHUNKS):
        priors.append(scatter_prior(chunk))

    parity = jnp.reshape((me & 1) * centres, (1,)).astype(jnp.int32)
    ydt, solved, ysum = pl.pallas_call(
        functools.partial(prepare_kernel, count, rows, width, obs_len),
        grid_spec=pltpu.PrefetchScalarGridSpec(
            num_scalar_prefetch=1,
            grid=(1,),
            in_specs=[whole((2, rows, pair_width))] * count,
            out_specs=[
                whole((width + PAD_ROWS, members)),
                whole((members, width)),
                whole((width, span)),
            ],
        ),
        out_shape=[
            jax.ShapeDtypeStruct((width + PAD_ROWS, members), jnp.bfloat16),
            jax.ShapeDtypeStruct((members, width), jnp.bfloat16),
            jax.ShapeDtypeStruct((width, span), jnp.float32),
        ],
        compiler_params=pltpu.CompilerParams(vmem_limit_bytes=VMEM_BYTES),
        cost_estimate=pl.CostEstimate(
            flops=20 * members * width, bytes_accessed=8 * members * width, transcendentals=0
        ),
    )(parity, *pieces)

    taper = jnp.transpose(localisation_matrix, (0, 2, 1)) * (1.0 / (members - 1))
    first_block = strip_position * band_blocks + me * centres - RIM_BLOCKS
    start = me * per_worker
    blocks = lax.dynamic_slice_in_dim(measurement_group_matrix, start, per_worker, 0) - first_block
    tapers = lax.dynamic_slice_in_dim(localisation_factors, start, per_worker, 0)

    step_span = STEP_PATCHES * span
    piece_spec = pl.BlockSpec((rows, step_span), lambda i, *_: (0, i))

    def analyse(chunk, prior):
        mine = slice(chunk * chunk_patches, (chunk + 1) * chunk_patches)
        *out, variance = pl.pallas_call(
            functools.partial(analyse_kernel, count, rows, span, obs_len, nblk),
            grid_spec=pltpu.PrefetchScalarGridSpec(
                num_scalar_prefetch=2,
                grid=(chunk_patches // STEP_PATCHES,),
                in_specs=[piece_spec] * count
                + [
                    whole((width + PAD_ROWS, members)),
                    whole((members, width)),
                    whole((width, span)),
                    whole((taper_count, obs_len, span)),
                ],
                out_specs=[piece_spec] * count + [whole((chunk_patches, span))],
                scratch_shapes=[pltpu.VMEM((width, step_span), jnp.float32)],
            ),
            out_shape=[jax.ShapeDtypeStruct((rows, chunk_span), jnp.bfloat16)] * count
            + [jax.ShapeDtypeStruct((chunk_patches, span), jnp.float32)],
            compiler_params=pltpu.CompilerParams(vmem_limit_bytes=VMEM_BYTES),
            cost_estimate=pl.CostEstimate(
                flops=4 * members * width * chunk_span,
                bytes_accessed=4 * members * (width + chunk_span),
                transcendentals=0,
            ),
        )(blocks[mine].reshape(-1), tapers[mine].reshape(-1), *prior, ydt, solved, ysum, taper)
        return out, variance

    analysis = jnp.zeros(prior_ensemble.shape, prior_ensemble.dtype)
    variances = []
    for chunk in range(CHUNKS):
        out, variance = analyse(chunk, priors[chunk])
        variances.append(variance)
        for flip in order + [0]:
            piece = partner(out[flip], flip) if flip else out[0]
            first = (me ^ flip) * (per_worker * span) + chunk * chunk_span
            analysis = lax.dynamic_update_slice(analysis, piece, (0, first))

    gathered = jnp.concatenate(variances, axis=0)
    flip = 1
    while flip < count:
        gathered = jnp.concatenate([gathered, partner(gathered, flip)], axis=0)
        flip *= 2
    spread = pl.pallas_call(
        functools.partial(spread_kernel, per_worker),
        grid_spec=pltpu.PrefetchScalarGridSpec(
            num_scalar_prefetch=2,
            grid=(1,),
            in_specs=[whole((strip, span))],
            out_specs=whole((2 * per_worker, span)),
        ),
        out_shape=jax.ShapeDtypeStruct((2 * per_worker, span), jnp.float32),
    )(piece_owner_device, jnp.reshape(me, (1,)).astype(jnp.int32), gathered)
    return analysis, spread


def solution(mesh):
    return jax.shard_map(
        per_device,
        mesh=mesh,
        in_specs=(
            P("mem", "band"),
            P("mem", "band"),
            P("mem", "band"),
            P(),
            P("band"),
            P("band", None),
            P("band", None),
        ),
        out_specs=(P("mem", "band"), P(("band", "mem"), None)),
        check_vma=False,
    )
```

```python
import functools

import jax
import jax.numpy as jnp
from jax import lax
from jax.experimental import pallas as pl
from jax.experimental.pallas import tpu as pltpu
from jax.sharding import PartitionSpec as P

RIM_BLOCKS = 2
CHUNKS = 2
STEP_PATCHES = 4
PAD_ROWS = 16
VMEM_BYTES = 60 * 1024 * 1024
IN_FLIGHT = 4
FIRST = 3
EARLY = 3
ASSEMBLE_BEFORE = 4


def taper_kernel(scale, loc_ref, taper_ref):
    for i in range(loc_ref.shape[0]):
        taper_ref[i] = jnp.transpose(loc_ref[i]) * scale


def assemble_kernel(moves, span, place_ref, *refs):
    pieces, (out_ref, sems) = refs[: len(moves)], refs[-2:]
    copies = []
    for i, (flip, stride, first) in enumerate(moves):
        column = jnp.bitwise_xor(place_ref[0], flip) * stride + first
        there = out_ref.at[:, pl.ds(pl.multiple_of(column, span), pieces[i].shape[1])]
        copies.append(pltpu.make_async_copy(pieces[i], there, sems.at[i]))
        copies[-1].start()
    for copy in copies:
        copy.wait()


def prepare_kernel(count, rows, width, centres, obs_len, place_ref, *refs):
    pieces, (ydt_ref, solved_ref, ysum_ref) = refs[:count], refs[count:]
    offset = pl.multiple_of((place_ref[0] & 1) * (centres * obs_len), obs_len)
    window = pl.ds(offset, width)
    members = count * rows
    total = jnp.zeros((1, width), jnp.float32)
    for piece in pieces:
        total = total + jnp.sum(piece[0, :, window].astype(jnp.float32), axis=0, keepdims=True)
    centre = total / members
    for i, piece in enumerate(pieces):
        place = slice(i * rows, (i + 1) * rows)
        dev = piece[0, :, window].astype(jnp.float32) - centre
        ydt_ref[:width, place] = jnp.transpose(dev).astype(jnp.bfloat16)
        solved_ref[place, :] = piece[1, :, window]
    ydt_ref[width:, :] = jnp.ones((ydt_ref.shape[0] - width, members), jnp.bfloat16)
    ysum_ref[...] = jnp.dot(
        ydt_ref[:width, :],
        jnp.ones((members, ysum_ref.shape[1]), jnp.bfloat16),
        preferred_element_type=jnp.float32,
    )


def analyse_kernel(count, rows, span, obs_len, start, geometry, place_ref, block_ref, taper_ref, *refs):
    priors, (ydt_ref, solved_ref, ysum_ref, loc_ref) = refs[:count], refs[count : count + 4]
    outs, (var_ref, weight_ref) = refs[count + 4 : 2 * count + 4], refs[2 * count + 4 :]
    step = pl.program_id(0)
    per_worker, centres, band_blocks = geometry
    first_patch = place_ref[0] * per_worker + start
    first_block = place_ref[1] * band_blocks + place_ref[0] * centres - RIM_BLOCKS
    width = solved_ref.shape[1]
    members = count * rows
    patches = priors[0].shape[1] // span
    weight_ref[...] = jnp.zeros_like(weight_ref)
    for j in range(patches):
        patch = first_patch + step * patches + j
        for k in range(block_ref.shape[0]):
            row = pl.multiple_of((block_ref[k, patch] - first_block) * obs_len, obs_len)
            there = (pl.ds(row, obs_len), slice(j * span, (j + 1) * span))
            weight_ref[there] = weight_ref[there] + loc_ref[taper_ref[k, patch]]
    prior = jnp.concatenate([ref[...] for ref in priors], axis=0)
    product = jnp.dot(ydt_ref[...], prior, preferred_element_type=jnp.float32)
    mean = product[width : width + 1, :] * (1.0 / members)
    ysum = jnp.concatenate([ysum_ref[...]] * patches, axis=1)
    cov = product[:width, :] - ysum * mean
    tapered = (cov * weight_ref[...]).astype(jnp.bfloat16)
    increment = jnp.dot(solved_ref[...], tapered, preferred_element_type=jnp.float32)
    updated = (prior.astype(jnp.float32) + increment).astype(jnp.bfloat16)
    for i, out in enumerate(outs):
        out[...] = updated[i * rows : (i + 1) * rows, :]
    updated = updated.astype(jnp.float32)
    centre = jnp.sum(updated, axis=0, keepdims=True) * (1.0 / members)
    variance = jnp.sum((updated - centre) ** 2, axis=0, keepdims=True) * (1.0 / members)
    for j in range(patches):
        var_ref[pl.ds(step * patches + j, 1), :] = variance[:, j * span : (j + 1) * span]


def select_kernel(per_worker, owner_ref, place_ref, out_ref):
    me = place_ref[0]
    out_ref[...] = jnp.zeros_like(out_ref)
    lanes = lax.broadcasted_iota(jnp.int32, (1, out_ref.shape[1]), 1)

    def one(patch, filled):
        mine = owner_ref[patch] == me

        @pl.when(mine)
        def _():
            source = jnp.bitwise_xor(patch // per_worker, me) * per_worker + patch % per_worker
            out_ref[pl.ds(filled, 1), :] = (lanes == source).astype(jnp.float32)

        return filled + mine.astype(jnp.int32)

    lax.fori_loop(0, owner_ref.shape[0], one, jnp.int32(0))


def spread_kernel(select_ref, var_ref, out_ref):
    out_ref[...] = jnp.dot(
        select_ref[...],
        var_ref[...],
        precision=lax.Precision.HIGHEST,
        preferred_element_type=jnp.float32,
    )


def whole(shape):
    return pl.BlockSpec(shape, lambda *_: (0,) * len(shape))


def per_device(
    prior_ensemble,
    perturbed_measurements,
    solved_residuals,
    localisation_matrix,
    piece_owner_device,
    measurement_group_matrix,
    localisation_factors,
):
    rows, vector_span = prior_ensemble.shape
    taper_count, span, obs_len = localisation_matrix.shape
    count, bands = lax.axis_size("mem"), lax.axis_size("band")
    members = rows * count
    strip = vector_span // span
    band_blocks = perturbed_measurements.shape[1] // obs_len
    per_worker = strip // count
    centres = per_worker * band_blocks // strip
    assert centres * strip == per_worker * band_blocks and count & (count - 1) == 0
    window = 2 * RIM_BLOCKS + centres
    width = window * obs_len
    strip_position = lax.axis_index("band")
    me = lax.axis_index("mem")

    place = jnp.stack([me, strip_position]).astype(jnp.int32)
    sent = []

    def after_sent(x):
        if len(sent) >= IN_FLIGHT:
            x, sent[-IN_FLIGHT] = lax.optimization_barrier((x, sent[-IN_FLIGHT]))
        return x

    def partner(x, flip):
        pairs = [(i, i ^ flip) for i in range(count)]
        if flip == 1:
            return lax.ppermute(x, "mem", pairs)
        sent.append(lax.ppermute(after_sent(x), "mem", pairs))
        return sent[-1]

    pair_width = (window + centres) * obs_len

    chunk_patches = per_worker // CHUNKS
    chunk_span = chunk_patches * span

    select = pl.pallas_call(
        functools.partial(select_kernel, per_worker),
        grid_spec=pltpu.PrefetchScalarGridSpec(
            num_scalar_prefetch=2,
            grid=(1,),
            in_specs=[],
            out_specs=whole((2 * per_worker, strip)),
        ),
        out_shape=jax.ShapeDtypeStruct((2 * per_worker, strip), jnp.float32),
    )(piece_owner_device, place)
    taper = pl.pallas_call(
        functools.partial(taper_kernel, 1.0 / (members - 1)),
        out_shape=jax.ShapeDtypeStruct((taper_count, obs_len, span), jnp.float32),
        compiler_params=pltpu.CompilerParams(vmem_limit_bytes=VMEM_BYTES),
    )(localisation_matrix)

    order = list(range(2, count, 2)) + list(range(3, count, 2)) + [1]

    def outgoing(source, flip, chunk):
        first = (me ^ flip) * (per_worker * span) + chunk * chunk_span
        return lax.dynamic_slice_in_dim(source, first, chunk_span, 1)

    source, cut = prior_ensemble, []
    got = [{} for _ in range(CHUNKS)]
    for flip in order[:FIRST]:
        cut.append(outgoing(source, flip, 0))
        source, cut[-1] = lax.optimization_barrier((source, cut[-1]))
        got[0][flip] = partner(cut[-1], flip)
    both = jnp.stack([perturbed_measurements, solved_residuals])
    both, got[0][order[0]] = lax.optimization_barrier((both, got[0][order[0]]))
    up = [(i, i + 1) for i in range(bands - 1)]
    down = [(j, i) for i, j in up]
    rim = RIM_BLOCKS * obs_len
    before = lax.ppermute(both[:, :, -rim:], "band", up)
    after = lax.ppermute(both[:, :, :rim], "band", down)
    padded = jnp.concatenate([before, both, after], axis=2)

    def pair_window(flip):
        first = ((me ^ flip) >> 1) * (2 * centres * obs_len)
        return lax.dynamic_slice_in_dim(padded, first, pair_width, 2)

    for flip in order[FIRST:]:
        got[0][flip] = partner(outgoing(source, flip, 0), flip)
    even = {0: pair_window(0)}
    for flip in range(2, count, 2):
        even[flip] = partner(pair_window(flip), flip)
    for flip in order[:EARLY]:
        got[1][flip] = partner(outgoing(source, flip, 1), flip)
    even[0], select, taper = lax.optimization_barrier((even[0], select, taper))
    pieces = []
    for flip in range(0, count, 2):
        pieces += [even[flip], partner(even[flip], 1)]
    for chunk in range(1, CHUNKS):
        for flip in order:
            if flip not in got[chunk]:
                got[chunk][flip] = partner(outgoing(source, flip, chunk), flip)
    priors = [[pieces_of[i] for i in range(1, count)] for pieces_of in got]

    ydt, solved, ysum = pl.pallas_call(
        functools.partial(prepare_kernel, count, rows, width, centres, obs_len),
        grid_spec=pltpu.PrefetchScalarGridSpec(
            num_scalar_prefetch=1,
            grid=(1,),
            in_specs=[whole((2, rows, pair_width))] * count,
            out_specs=[
                whole((width + PAD_ROWS, members)),
                whole((members, width)),
                whole((width, span)),
            ],
        ),
        out_shape=[
            jax.ShapeDtypeStruct((width + PAD_ROWS, members), jnp.bfloat16),
            jax.ShapeDtypeStruct((members, width), jnp.bfloat16),
            jax.ShapeDtypeStruct((width, span), jnp.float32),
        ],
        compiler_params=pltpu.CompilerParams(vmem_limit_bytes=VMEM_BYTES),
        cost_estimate=pl.CostEstimate(
            flops=20 * members * width, bytes_accessed=8 * members * width, transcendentals=0
        ),
    )(place, *pieces)

    step_span = STEP_PATCHES * span
    piece_spec = pl.BlockSpec((rows, step_span), lambda i, *_: (0, i))
    blocks, tapers = measurement_group_matrix.T, localisation_factors.T

    def analyse(chunk, prior):
        steps = chunk_patches // STEP_PATCHES

        def own(i, place_ref, *_):
            return 0, (place_ref[0] * CHUNKS + chunk) * steps + i

        *out, variance = pl.pallas_call(
            functools.partial(
                analyse_kernel,
                count,
                rows,
                span,
                obs_len,
                chunk * chunk_patches,
                (per_worker, centres, band_blocks),
            ),
            grid_spec=pltpu.PrefetchScalarGridSpec(
                num_scalar_prefetch=3,
                grid=(steps,),
                in_specs=[pl.BlockSpec((rows, step_span), own)]
                + [piece_spec] * (count - 1)
                + [
                    whole((width + PAD_ROWS, members)),
                    whole((members, width)),
                    whole((width, span)),
                    whole((taper_count, obs_len, span)),
                ],
                out_specs=[piece_spec] * count + [whole((chunk_patches, span))],
                scratch_shapes=[pltpu.VMEM((width, step_span), jnp.float32)],
            ),
            out_shape=[jax.ShapeDtypeStruct((rows, chunk_span), jnp.bfloat16)] * count
            + [jax.ShapeDtypeStruct((chunk_patches, span), jnp.float32)],
            compiler_params=pltpu.CompilerParams(vmem_limit_bytes=VMEM_BYTES),
            cost_estimate=pl.CostEstimate(
                flops=4 * members * width * chunk_span,
                bytes_accessed=4 * members * (width + chunk_span),
                transcendentals=0,
            ),
        )(place, blocks, tapers, prior_ensemble, *prior, ydt, solved, ysum, taper)
        return out, variance

    def assemble(analysis, pieces, moves):
        base = [] if analysis is None else [analysis]
        return pl.pallas_call(
            functools.partial(assemble_kernel, moves, span),
            grid_spec=pltpu.PrefetchScalarGridSpec(
                num_scalar_prefetch=1,
                grid=(1,),
                in_specs=[whole((rows, chunk_span))] * len(pieces)
                + [pl.BlockSpec(memory_space=pl.ANY)] * len(base),
                out_specs=pl.BlockSpec(memory_space=pl.ANY),
                scratch_shapes=[pltpu.SemaphoreType.DMA((len(pieces),))],
            ),
            out_shape=jax.ShapeDtypeStruct(prior_ensemble.shape, prior_ensemble.dtype),
            input_output_aliases={1 + len(pieces): 0} if base else {},
            compiler_params=pltpu.CompilerParams(vmem_limit_bytes=VMEM_BYTES),
            cost_estimate=pl.CostEstimate(
                flops=0, bytes_accessed=4 * len(pieces) * rows * chunk_span, transcendentals=0
            ),
        )(place, *pieces, *base)

    analysis = None
    gathered, spread_flip = [], 1
    back = order
    for chunk in range(CHUNKS):
        out, variance = analyse(chunk, priors[chunk])
        gathered.append(variance)
        final = chunk == CHUNKS - 1
        arrived, moves = [], []
        for i, flip in enumerate([0] + back):
            if final and spread_flip < count:
                if spread_flip == 1:
                    gathered = jnp.concatenate(gathered, axis=0)
                gathered = jnp.concatenate([gathered, partner(gathered, spread_flip)], axis=0)
                spread_flip *= 2
            if final and i == ASSEMBLE_BEFORE:
                out[flip], analysis = lax.optimization_barrier((out[flip], analysis))
            arrived.append(partner(out[flip], flip) if flip else out[0])
            moves.append((flip, per_worker * span, chunk * chunk_span))
            if len(moves) == count or (final and len(moves) == count // 2 + 1):
                analysis = assemble(analysis, arrived, tuple(moves))
                arrived, moves = [], []
        if moves:
            analysis = assemble(analysis, arrived, tuple(moves))
    assert spread_flip == count
    spread = pl.pallas_call(
        spread_kernel,
        out_shape=jax.ShapeDtypeStruct((2 * per_worker, span), jnp.float32),
    )(select, gathered)
    return analysis, spread


def solution(mesh):
    return jax.shard_map(
        per_device,
        mesh=mesh,
        in_specs=(
            P("mem", "band"),
            P("mem", "band"),
            P("mem", "band"),
            P(),
            P("band"),
            P("band", None),
            P("band", None),
        ),
        out_specs=(P("mem", "band"), P(("band", "mem"), None)),
        check_vma=False,
    )
```

```python
import functools

import jax
import jax.numpy as jnp
from jax import lax
from jax.experimental import pallas as pl
from jax.experimental.pallas import tpu as pltpu
from jax.sharding import PartitionSpec as P

RIM_BLOCKS = 2
CHUNKS = 2
STEP_PATCHES = 4
PAD_ROWS = 16
VMEM_BYTES = 60 * 1024 * 1024
IN_FLIGHT = 4
FIRST = 4
EARLY = 3
ASSEMBLE_BEFORE = 4


def taper_kernel(scale, loc_ref, taper_ref):
    for i in range(loc_ref.shape[0]):
        taper_ref[i] = jnp.transpose(loc_ref[i]) * scale


def assemble_kernel(moves, span, place_ref, *refs):
    pieces, (out_ref, sems) = refs[: len(moves)], refs[-2:]
    copies = []
    for i, (flip, stride, first) in enumerate(moves):
        column = jnp.bitwise_xor(place_ref[0], flip) * stride + first
        there = out_ref.at[:, pl.ds(pl.multiple_of(column, span), pieces[i].shape[1])]
        copies.append(pltpu.make_async_copy(pieces[i], there, sems.at[i]))
        copies[-1].start()
    for copy in copies:
        copy.wait()


def prepare_kernel(count, rows, width, centres, obs_len, place_ref, *refs):
    pieces, (ydt_ref, solved_ref, ysum_ref) = refs[:count], refs[count:]
    offset = pl.multiple_of((place_ref[0] & 1) * (centres * obs_len), obs_len)
    window = pl.ds(offset, width)
    members = count * rows
    total = jnp.zeros((1, width), jnp.float32)
    for piece in pieces:
        total = total + jnp.sum(piece[0, :, window].astype(jnp.float32), axis=0, keepdims=True)
    centre = total / members
    for i, piece in enumerate(pieces):
        place = slice(i * rows, (i + 1) * rows)
        dev = piece[0, :, window].astype(jnp.float32) - centre
        ydt_ref[:width, place] = jnp.transpose(dev).astype(jnp.bfloat16)
        solved_ref[place, :] = piece[1, :, window]
    ydt_ref[width:, :] = jnp.ones((ydt_ref.shape[0] - width, members), jnp.bfloat16)
    ysum_ref[...] = jnp.dot(
        ydt_ref[:width, :],
        jnp.ones((members, ysum_ref.shape[1]), jnp.bfloat16),
        preferred_element_type=jnp.float32,
    )


def analyse_kernel(count, rows, span, obs_len, start, geometry, place_ref, block_ref, taper_ref, *refs):
    priors, (ydt_ref, solved_ref, ysum_ref, loc_ref) = refs[:count], refs[count : count + 4]
    outs, (var_ref, weight_ref) = refs[count + 4 : 2 * count + 4], refs[2 * count + 4 :]
    step = pl.program_id(0)
    per_worker, centres, band_blocks = geometry
    first_patch = place_ref[0] * per_worker + start
    first_block = place_ref[1] * band_blocks + place_ref[0] * centres - RIM_BLOCKS
    width = solved_ref.shape[1]
    members = count * rows
    patches = priors[0].shape[1] // span
    weight_ref[...] = jnp.zeros_like(weight_ref)
    for j in range(patches):
        patch = first_patch + step * patches + j
        for k in range(block_ref.shape[0]):
            row = pl.multiple_of((block_ref[k, patch] - first_block) * obs_len, obs_len)
            there = (pl.ds(row, obs_len), slice(j * span, (j + 1) * span))
            weight_ref[there] = weight_ref[there] + loc_ref[taper_ref[k, patch]]
    prior = jnp.concatenate([ref[...] for ref in priors], axis=0)
    product = jnp.dot(ydt_ref[...], prior, preferred_element_type=jnp.float32)
    mean = product[width : width + 1, :] * (1.0 / members)
    ysum = jnp.concatenate([ysum_ref[...]] * patches, axis=1)
    cov = product[:width, :] - ysum * mean
    tapered = (cov * weight_ref[...]).astype(jnp.bfloat16)
    increment = jnp.dot(solved_ref[...], tapered, preferred_element_type=jnp.float32)
    updated = (prior.astype(jnp.float32) + increment).astype(jnp.bfloat16)
    for i, out in enumerate(outs):
        out[...] = updated[i * rows : (i + 1) * rows, :]
    updated = updated.astype(jnp.float32)
    centre = jnp.sum(updated, axis=0, keepdims=True) * (1.0 / members)
    variance = jnp.sum((updated - centre) ** 2, axis=0, keepdims=True) * (1.0 / members)
    for j in range(patches):
        var_ref[pl.ds(step * patches + j, 1), :] = variance[:, j * span : (j + 1) * span]


def select_kernel(per_worker, owner_ref, place_ref, out_ref):
    me = place_ref[0]
    out_ref[...] = jnp.zeros_like(out_ref)
    lanes = lax.broadcasted_iota(jnp.int32, (1, out_ref.shape[1]), 1)

    def one(patch, filled):
        mine = owner_ref[patch] == me

        @pl.when(mine)
        def _():
            source = jnp.bitwise_xor(patch // per_worker, me) * per_worker + patch % per_worker
            out_ref[pl.ds(filled, 1), :] = (lanes == source).astype(jnp.float32)

        return filled + mine.astype(jnp.int32)

    lax.fori_loop(0, owner_ref.shape[0], one, jnp.int32(0))


def spread_kernel(select_ref, var_ref, out_ref):
    out_ref[...] = jnp.dot(
        select_ref[...],
        var_ref[...],
        precision=lax.Precision.HIGHEST,
        preferred_element_type=jnp.float32,
    )


def whole(shape):
    return pl.BlockSpec(shape, lambda *_: (0,) * len(shape))


def per_device(
    prior_ensemble,
    perturbed_measurements,
    solved_residuals,
    localisation_matrix,
    piece_owner_device,
    measurement_group_matrix,
    localisation_factors,
):
    rows, vector_span = prior_ensemble.shape
    taper_count, span, obs_len = localisation_matrix.shape
    count, bands = lax.axis_size("mem"), lax.axis_size("band")
    members = rows * count
    strip = vector_span // span
    band_blocks = perturbed_measurements.shape[1] // obs_len
    per_worker = strip // count
    centres = per_worker * band_blocks // strip
    assert centres * strip == per_worker * band_blocks and count & (count - 1) == 0
    window = 2 * RIM_BLOCKS + centres
    width = window * obs_len
    strip_position = lax.axis_index("band")
    me = lax.axis_index("mem")

    place = jnp.stack([me, strip_position]).astype(jnp.int32)
    sent = []

    def after_sent(x):
        if len(sent) >= IN_FLIGHT:
            x, sent[-IN_FLIGHT] = lax.optimization_barrier((x, sent[-IN_FLIGHT]))
        return x

    def partner(x, flip, after=()):
        if after:
            x = lax.optimization_barrier((x, *after))[0]
        pairs = [(i, i ^ flip) for i in range(count)]
        if flip == 1:
            return lax.ppermute(x, "mem", pairs)
        sent.append(lax.ppermute(after_sent(x), "mem", pairs))
        return sent[-1]

    pair_width = (window + centres) * obs_len

    chunk_patches = per_worker // CHUNKS
    chunk_span = chunk_patches * span

    select = pl.pallas_call(
        functools.partial(select_kernel, per_worker),
        grid_spec=pltpu.PrefetchScalarGridSpec(
            num_scalar_prefetch=2,
            grid=(1,),
            in_specs=[],
            out_specs=whole((2 * per_worker, strip)),
        ),
        out_shape=jax.ShapeDtypeStruct((2 * per_worker, strip), jnp.float32),
    )(piece_owner_device, place)
    taper = pl.pallas_call(
        functools.partial(taper_kernel, 1.0 / (members - 1)),
        out_shape=jax.ShapeDtypeStruct((taper_count, obs_len, span), jnp.float32),
        compiler_params=pltpu.CompilerParams(vmem_limit_bytes=VMEM_BYTES),
    )(localisation_matrix)

    order = list(range(2, count, 2)) + list(range(3, count, 2)) + [1]

    def outgoing(source, flip, chunk):
        first = (me ^ flip) * (per_worker * span) + chunk * chunk_span
        return lax.dynamic_slice_in_dim(source, first, chunk_span, 1)

    source, cut = prior_ensemble, []
    got = [{} for _ in range(CHUNKS)]
    for flip in order[:FIRST]:
        cut.append(outgoing(source, flip, 0))
        source, cut[-1] = lax.optimization_barrier((source, cut[-1]))
        got[0][flip] = partner(cut[-1], flip)
    both = jnp.stack([perturbed_measurements, solved_residuals])
    both, got[0][order[0]] = lax.optimization_barrier((both, got[0][order[0]]))
    up = [(i, i + 1) for i in range(bands - 1)]
    down = [(j, i) for i, j in up]
    rim = RIM_BLOCKS * obs_len
    before = lax.ppermute(both[:, :, -rim:], "band", up)
    after = lax.ppermute(both[:, :, :rim], "band", down)
    padded = jnp.concatenate([before, both, after], axis=2)

    def pair_window(flip):
        first = ((me ^ flip) >> 1) * (2 * centres * obs_len)
        return lax.dynamic_slice_in_dim(padded, first, pair_width, 2)

    for flip in order[FIRST:]:
        got[0][flip] = partner(outgoing(source, flip, 0), flip)
    even = {0: pair_window(0)}
    for flip in range(2, count, 2):
        even[flip] = partner(pair_window(flip), flip)
    for flip in order[:EARLY]:
        got[1][flip] = partner(outgoing(source, flip, 1), flip)
    even[0], select, taper = lax.optimization_barrier((even[0], select, taper))
    pieces = []
    for flip in range(0, count, 2):
        pieces += [even[flip], partner(even[flip], 1)]
    for chunk in range(1, CHUNKS):
        for flip in order:
            if flip not in got[chunk]:
                after = [pieces[flip - 2]] if chunk == 1 and flip & 1 and flip > 1 else []
                got[chunk][flip] = partner(outgoing(source, flip, chunk), flip, after)
    priors = [[pieces_of[i] for i in range(1, count)] for pieces_of in got]

    ydt, solved, ysum = pl.pallas_call(
        functools.partial(prepare_kernel, count, rows, width, centres, obs_len),
        grid_spec=pltpu.PrefetchScalarGridSpec(
            num_scalar_prefetch=1,
            grid=(1,),
            in_specs=[whole((2, rows, pair_width))] * count,
            out_specs=[
                whole((width + PAD_ROWS, members)),
                whole((members, width)),
                whole((width, span)),
            ],
        ),
        out_shape=[
            jax.ShapeDtypeStruct((width + PAD_ROWS, members), jnp.bfloat16),
            jax.ShapeDtypeStruct((members, width), jnp.bfloat16),
            jax.ShapeDtypeStruct((width, span), jnp.float32),
        ],
        compiler_params=pltpu.CompilerParams(vmem_limit_bytes=VMEM_BYTES),
    )(place, *pieces)

    step_span = STEP_PATCHES * span
    piece_spec = pl.BlockSpec((rows, step_span), lambda i, *_: (0, i))
    blocks, tapers = measurement_group_matrix.T, localisation_factors.T

    def analyse(chunk, prior):
        steps = chunk_patches // STEP_PATCHES

        def own(i, place_ref, *_):
            return 0, (place_ref[0] * CHUNKS + chunk) * steps + i

        *out, variance = pl.pallas_call(
            functools.partial(
                analyse_kernel,
                count,
                rows,
                span,
                obs_len,
                chunk * chunk_patches,
                (per_worker, centres, band_blocks),
            ),
            grid_spec=pltpu.PrefetchScalarGridSpec(
                num_scalar_prefetch=3,
                grid=(steps,),
                in_specs=[pl.BlockSpec((rows, step_span), own)]
                + [piece_spec] * (count - 1)
                + [
                    whole((width + PAD_ROWS, members)),
                    whole((members, width)),
                    whole((width, span)),
                    whole((taper_count, obs_len, span)),
                ],
                out_specs=[piece_spec] * count + [whole((chunk_patches, span))],
                scratch_shapes=[pltpu.VMEM((width, step_span), jnp.float32)],
            ),
            out_shape=[jax.ShapeDtypeStruct((rows, chunk_span), jnp.bfloat16)] * count
            + [jax.ShapeDtypeStruct((chunk_patches, span), jnp.float32)],
            compiler_params=pltpu.CompilerParams(vmem_limit_bytes=VMEM_BYTES),
        )(place, blocks, tapers, prior_ensemble, *prior, ydt, solved, ysum, taper)
        return out, variance

    def assemble(analysis, pieces, moves):
        base = [] if analysis is None else [analysis]
        return pl.pallas_call(
            functools.partial(assemble_kernel, moves, span),
            grid_spec=pltpu.PrefetchScalarGridSpec(
                num_scalar_prefetch=1,
                grid=(1,),
                in_specs=[whole((rows, chunk_span))] * len(pieces)
                + [pl.BlockSpec(memory_space=pl.ANY)] * len(base),
                out_specs=pl.BlockSpec(memory_space=pl.ANY),
                scratch_shapes=[pltpu.SemaphoreType.DMA((len(pieces),))],
            ),
            out_shape=jax.ShapeDtypeStruct(prior_ensemble.shape, prior_ensemble.dtype),
            input_output_aliases={1 + len(pieces): 0} if base else {},
            compiler_params=pltpu.CompilerParams(vmem_limit_bytes=VMEM_BYTES),
        )(place, *pieces, *base)

    analysis = None
    gathered, spread_flip = [], 1
    back = order
    for chunk in range(CHUNKS):
        out, variance = analyse(chunk, priors[chunk])
        gathered.append(variance)
        final = chunk == CHUNKS - 1
        arrived, moves = [], []
        for i, flip in enumerate([0] + back):
            if final and spread_flip < count:
                if spread_flip == 1:
                    gathered = jnp.concatenate(gathered, axis=0)
                gathered = jnp.concatenate([gathered, partner(gathered, spread_flip)], axis=0)
                spread_flip *= 2
            if final and i == ASSEMBLE_BEFORE:
                out[flip], analysis = lax.optimization_barrier((out[flip], analysis))
            arrived.append(partner(out[flip], flip) if flip else out[0])
            moves.append((flip, per_worker * span, chunk * chunk_span))
            if len(moves) == count or (final and len(moves) == count // 2 + 1):
                analysis = assemble(analysis, arrived, tuple(moves))
                arrived, moves = [], []
        if moves:
            analysis = assemble(analysis, arrived, tuple(moves))
    assert spread_flip == count
    spread = pl.pallas_call(
        spread_kernel,
        out_shape=jax.ShapeDtypeStruct((2 * per_worker, span), jnp.float32),
    )(select, gathered)
    return analysis, spread


def solution(mesh):
    return jax.shard_map(
        per_device,
        mesh=mesh,
        in_specs=(
            P("mem", "band"),
            P("mem", "band"),
            P("mem", "band"),
            P(),
            P("band"),
            P("band", None),
            P("band", None),
        ),
        out_specs=(P("mem", "band"), P(("band", "mem"), None)),
        check_vma=False,
    )
```

```python
import functools

import jax
import jax.numpy as jnp
from jax import lax
from jax.experimental import pallas as pl
from jax.experimental.pallas import tpu as pltpu
from jax.sharding import PartitionSpec as P

RIM_BLOCKS = 2
CHUNKS = 2
STEP_PATCHES = 8
PAD_ROWS = 16
VMEM_BYTES = 60 * 1024 * 1024
IN_FLIGHT = 4
FIRST = 4
ASSEMBLE_BYTES = 8 * 1024 * 1024
EARLY = 3
ASSEMBLE_BEFORE = 4


def taper_kernel(scale, loc_ref, taper_ref):
    for i in range(loc_ref.shape[0]):
        taper_ref[i] = jnp.transpose(loc_ref[i]) * scale


def assemble_kernel(moves, span, place_ref, *refs):
    pieces, (out_ref, sems) = refs[: len(moves)], refs[-2:]
    copies = []
    for i, (flip, stride, first) in enumerate(moves):
        column = jnp.bitwise_xor(place_ref[0], flip) * stride + first
        there = out_ref.at[:, pl.ds(pl.multiple_of(column, span), pieces[i].shape[1])]
        copies.append(pltpu.make_async_copy(pieces[i], there, sems.at[i]))
        copies[-1].start()
    for copy in copies:
        copy.wait()


def prepare_kernel(count, rows, width, centres, obs_len, place_ref, *refs):
    pieces, (ydt_ref, solved_ref, ysum_ref) = refs[:count], refs[count:]
    offset = pl.multiple_of((place_ref[0] & 1) * (centres * obs_len), obs_len)
    window = pl.ds(offset, width)
    members = count * rows
    total = jnp.zeros((1, width), jnp.float32)
    for piece in pieces:
        total = total + jnp.sum(piece[0, :, window].astype(jnp.float32), axis=0, keepdims=True)
    centre = total / members
    for i, piece in enumerate(pieces):
        place = slice(i * rows, (i + 1) * rows)
        dev = piece[0, :, window].astype(jnp.float32) - centre
        ydt_ref[:width, place] = jnp.transpose(dev).astype(jnp.bfloat16)
        solved_ref[place, :] = piece[1, :, window]
    ydt_ref[width:, :] = jnp.ones((ydt_ref.shape[0] - width, members), jnp.bfloat16)
    ysum_ref[...] = jnp.dot(
        ydt_ref[:width, :],
        jnp.ones((members, ysum_ref.shape[1]), jnp.bfloat16),
        preferred_element_type=jnp.float32,
    )


def analyse_kernel(count, rows, span, obs_len, start, geometry, place_ref, block_ref, taper_ref, *refs):
    priors, (ydt_ref, solved_ref, ysum_ref, loc_ref) = refs[:count], refs[count : count + 4]
    outs, (var_ref, weight_ref) = refs[count + 4 : 2 * count + 4], refs[2 * count + 4 :]
    step = pl.program_id(0)
    per_worker, centres, band_blocks = geometry
    first_patch = place_ref[0] * per_worker + start
    first_block = place_ref[1] * band_blocks + place_ref[0] * centres - RIM_BLOCKS
    width = solved_ref.shape[1]
    members = count * rows
    patches = priors[0].shape[1] // span
    weight_ref[...] = jnp.zeros_like(weight_ref)
    for j in range(patches):
        patch = first_patch + step * patches + j
        for k in range(block_ref.shape[0]):
            row = pl.multiple_of((block_ref[k, patch] - first_block) * obs_len, obs_len)
            there = (pl.ds(row, obs_len), slice(j * span, (j + 1) * span))
            weight_ref[there] = weight_ref[there] + loc_ref[taper_ref[k, patch]]
    prior = jnp.concatenate([ref[...] for ref in priors], axis=0)
    product = jnp.dot(ydt_ref[...], prior, preferred_element_type=jnp.float32)
    mean = product[width : width + 1, :] * (1.0 / members)
    ysum = jnp.concatenate([ysum_ref[...]] * patches, axis=1)
    cov = product[:width, :] - ysum * mean
    tapered = (cov * weight_ref[...]).astype(jnp.bfloat16)
    increment = jnp.dot(solved_ref[...], tapered, preferred_element_type=jnp.float32)
    updated = (prior.astype(jnp.float32) + increment).astype(jnp.bfloat16)
    for i, out in enumerate(outs):
        out[...] = updated[i * rows : (i + 1) * rows, :]
    updated = updated.astype(jnp.float32)
    centre = jnp.sum(updated, axis=0, keepdims=True) * (1.0 / members)
    variance = jnp.sum((updated - centre) ** 2, axis=0, keepdims=True) * (1.0 / members)
    for j in range(patches):
        var_ref[pl.ds(step * patches + j, 1), :] = variance[:, j * span : (j + 1) * span]


def select_kernel(per_worker, owner_ref, place_ref, out_ref):
    me = place_ref[0]
    out_ref[...] = jnp.zeros_like(out_ref)
    lanes = lax.broadcasted_iota(jnp.int32, (1, out_ref.shape[1]), 1)

    def one(patch, filled):
        mine = owner_ref[patch] == me

        @pl.when(mine)
        def _():
            source = jnp.bitwise_xor(patch // per_worker, me) * per_worker + patch % per_worker
            out_ref[pl.ds(filled, 1), :] = (lanes == source).astype(jnp.float32)

        return filled + mine.astype(jnp.int32)

    lax.fori_loop(0, owner_ref.shape[0], one, jnp.int32(0))


def spread_kernel(select_ref, var_ref, out_ref):
    out_ref[...] = jnp.dot(
        select_ref[...],
        var_ref[...],
        precision=lax.Precision.HIGHEST,
        preferred_element_type=jnp.float32,
    )


def whole(shape):
    return pl.BlockSpec(shape, lambda *_: (0,) * len(shape))


def per_device(
    prior_ensemble,
    perturbed_measurements,
    solved_residuals,
    localisation_matrix,
    piece_owner_device,
    measurement_group_matrix,
    localisation_factors,
):
    rows, vector_span = prior_ensemble.shape
    taper_count, span, obs_len = localisation_matrix.shape
    count, bands = lax.axis_size("mem"), lax.axis_size("band")
    members = rows * count
    strip = vector_span // span
    band_blocks = perturbed_measurements.shape[1] // obs_len
    per_worker = strip // count
    centres = per_worker * band_blocks // strip
    assert centres * strip == per_worker * band_blocks and count & (count - 1) == 0
    window = 2 * RIM_BLOCKS + centres
    width = window * obs_len
    strip_position = lax.axis_index("band")
    me = lax.axis_index("mem")

    place = jnp.stack([me, strip_position]).astype(jnp.int32)
    sent = []

    def after_sent(x):
        if len(sent) >= IN_FLIGHT:
            x, sent[-IN_FLIGHT] = lax.optimization_barrier((x, sent[-IN_FLIGHT]))
        return x

    def partner(x, flip, after=()):
        if after:
            x = lax.optimization_barrier((x, *after))[0]
        pairs = [(i, i ^ flip) for i in range(count)]
        if flip == 1:
            return lax.ppermute(x, "mem", pairs)
        sent.append(lax.ppermute(after_sent(x), "mem", pairs))
        return sent[-1]

    pair_width = (window + centres) * obs_len

    chunk_patches = per_worker // CHUNKS
    chunk_span = chunk_patches * span

    select = pl.pallas_call(
        functools.partial(select_kernel, per_worker),
        grid_spec=pltpu.PrefetchScalarGridSpec(
            num_scalar_prefetch=2,
            grid=(1,),
            in_specs=[],
            out_specs=whole((2 * per_worker, strip)),
        ),
        out_shape=jax.ShapeDtypeStruct((2 * per_worker, strip), jnp.float32),
    )(piece_owner_device, place)
    taper = pl.pallas_call(
        functools.partial(taper_kernel, 1.0 / (members - 1)),
        out_shape=jax.ShapeDtypeStruct((taper_count, obs_len, span), jnp.float32),
        compiler_params=pltpu.CompilerParams(vmem_limit_bytes=VMEM_BYTES),
    )(localisation_matrix)

    order = list(range(2, count, 2)) + list(range(3, count, 2)) + [1]

    def outgoing(source, flip, chunk):
        first = (me ^ flip) * (per_worker * span) + chunk * chunk_span
        return lax.dynamic_slice_in_dim(source, first, chunk_span, 1)

    source, cut = prior_ensemble, []
    got = [{} for _ in range(CHUNKS)]
    for flip in order[:FIRST]:
        cut.append(outgoing(source, flip, 0))
        source, cut[-1] = lax.optimization_barrier((source, cut[-1]))
        got[0][flip] = partner(cut[-1], flip)
    both = jnp.stack([perturbed_measurements, solved_residuals])
    both, got[0][order[0]] = lax.optimization_barrier((both, got[0][order[0]]))
    up = [(i, i + 1) for i in range(bands - 1)]
    down = [(j, i) for i, j in up]
    rim = RIM_BLOCKS * obs_len
    before = lax.ppermute(both[:, :, -rim:], "band", up)
    after = lax.ppermute(both[:, :, :rim], "band", down)
    padded = jnp.concatenate([before, both, after], axis=2)

    def pair_window(flip):
        first = ((me ^ flip) >> 1) * (2 * centres * obs_len)
        return lax.dynamic_slice_in_dim(padded, first, pair_width, 2)

    for flip in order[FIRST:]:
        got[0][flip] = partner(outgoing(source, flip, 0), flip)
    even = {0: pair_window(0)}
    for flip in range(2, count, 2):
        even[flip] = partner(pair_window(flip), flip)
    for flip in order[:EARLY]:
        got[1][flip] = partner(outgoing(source, flip, 1), flip)
    even[0], select, taper = lax.optimization_barrier((even[0], select, taper))
    pieces = []
    for flip in range(0, count, 2):
        pieces += [even[flip], partner(even[flip], 1)]
    for chunk in range(1, CHUNKS):
        for flip in order:
            if flip not in got[chunk]:
                after = [pieces[flip - 2]] if chunk == 1 and flip & 1 and flip > 1 else []
                got[chunk][flip] = partner(outgoing(source, flip, chunk), flip, after)
    priors = [[pieces_of[i] for i in range(1, count)] for pieces_of in got]

    ydt, solved, ysum = pl.pallas_call(
        functools.partial(prepare_kernel, count, rows, width, centres, obs_len),
        grid_spec=pltpu.PrefetchScalarGridSpec(
            num_scalar_prefetch=1,
            grid=(1,),
            in_specs=[whole((2, rows, pair_width))] * count,
            out_specs=[
                whole((width + PAD_ROWS, members)),
                whole((members, width)),
                whole((width, span)),
            ],
        ),
        out_shape=[
            jax.ShapeDtypeStruct((width + PAD_ROWS, members), jnp.bfloat16),
            jax.ShapeDtypeStruct((members, width), jnp.bfloat16),
            jax.ShapeDtypeStruct((width, span), jnp.float32),
        ],
        compiler_params=pltpu.CompilerParams(vmem_limit_bytes=VMEM_BYTES),
    )(place, *pieces)

    step_span = STEP_PATCHES * span
    piece_spec = pl.BlockSpec((rows, step_span), lambda i, *_: (0, i))
    blocks, tapers = measurement_group_matrix.T, localisation_factors.T

    def analyse(chunk, prior):
        steps = chunk_patches // STEP_PATCHES

        def own(i, place_ref, *_):
            return 0, (place_ref[0] * CHUNKS + chunk) * steps + i

        *out, variance = pl.pallas_call(
            functools.partial(
                analyse_kernel,
                count,
                rows,
                span,
                obs_len,
                chunk * chunk_patches,
                (per_worker, centres, band_blocks),
            ),
            grid_spec=pltpu.PrefetchScalarGridSpec(
                num_scalar_prefetch=3,
                grid=(steps,),
                in_specs=[pl.BlockSpec((rows, step_span), own)]
                + [piece_spec] * (count - 1)
                + [
                    whole((width + PAD_ROWS, members)),
                    whole((members, width)),
                    whole((width, span)),
                    whole((taper_count, obs_len, span)),
                ],
                out_specs=[piece_spec] * count + [whole((chunk_patches, span))],
                scratch_shapes=[pltpu.VMEM((width, step_span), jnp.float32)],
            ),
            out_shape=[jax.ShapeDtypeStruct((rows, chunk_span), jnp.bfloat16)] * count
            + [jax.ShapeDtypeStruct((chunk_patches, span), jnp.float32)],
            compiler_params=pltpu.CompilerParams(vmem_limit_bytes=VMEM_BYTES),
        )(place, blocks, tapers, prior_ensemble, *prior, ydt, solved, ysum, taper)
        return out, variance

    def assemble(analysis, pieces, moves):
        base = [] if analysis is None else [analysis]
        return pl.pallas_call(
            functools.partial(assemble_kernel, moves, span),
            grid_spec=pltpu.PrefetchScalarGridSpec(
                num_scalar_prefetch=1,
                grid=(1,),
                in_specs=[whole((rows, chunk_span))] * len(pieces)
                + [pl.BlockSpec(memory_space=pl.ANY)] * len(base),
                out_specs=pl.BlockSpec(memory_space=pl.ANY),
                scratch_shapes=[pltpu.SemaphoreType.DMA((len(pieces),))],
            ),
            out_shape=jax.ShapeDtypeStruct(prior_ensemble.shape, prior_ensemble.dtype),
            input_output_aliases={1 + len(pieces): 0} if base else {},
            compiler_params=pltpu.CompilerParams(vmem_limit_bytes=ASSEMBLE_BYTES if base else VMEM_BYTES),
        )(place, *pieces, *base)

    analysis = None
    gathered, spread_flip = [], 1
    back = order
    for chunk in range(CHUNKS):
        out, variance = analyse(chunk, priors[chunk])
        gathered.append(variance)
        final = chunk == CHUNKS - 1
        arrived, moves = [], []
        for i, flip in enumerate([0] + back):
            if final and spread_flip < count:
                if spread_flip == 1:
                    gathered = jnp.concatenate(gathered, axis=0)
                gathered = jnp.concatenate([gathered, partner(gathered, spread_flip)], axis=0)
                spread_flip *= 2
            if final and i == ASSEMBLE_BEFORE:
                out[flip], analysis = lax.optimization_barrier((out[flip], analysis))
            arrived.append(partner(out[flip], flip) if flip else out[0])
            moves.append((flip, per_worker * span, chunk * chunk_span))
            if len(moves) == count or (final and len(moves) == count // 2 + 1):
                analysis = assemble(analysis, arrived, tuple(moves))
                arrived, moves = [], []
        if moves:
            analysis = assemble(analysis, arrived, tuple(moves))
    assert spread_flip == count
    spread = pl.pallas_call(
        spread_kernel,
        out_shape=jax.ShapeDtypeStruct((2 * per_worker, span), jnp.float32),
    )(select, gathered)
    return analysis, spread


def solution(mesh):
    return jax.shard_map(
        per_device,
        mesh=mesh,
        in_specs=(
            P("mem", "band"),
            P("mem", "band"),
            P("mem", "band"),
            P(),
            P("band"),
            P("band", None),
            P("band", None),
        ),
        out_specs=(P("mem", "band"), P(("band", "mem"), None)),
        check_vma=False,
    )
```

```python
import functools

import jax
import jax.numpy as jnp
from jax import lax
from jax.experimental import pallas as pl
from jax.experimental.pallas import tpu as pltpu
from jax.sharding import PartitionSpec as P

RIM_BLOCKS = 2
CHUNKS = 2
STEP_PATCHES = 8
PAD_ROWS = 16
VMEM_BYTES = 60 * 1024 * 1024
IN_FLIGHT = 4
FIRST = 4
ASSEMBLE_BYTES = 8 * 1024 * 1024
EARLY = 3
ASSEMBLE_BEFORE = 4


def taper_kernel(scale, loc_ref, taper_ref):
    for i in range(loc_ref.shape[0]):
        taper_ref[i] = jnp.transpose(loc_ref[i]) * scale


def assemble_kernel(moves, span, place_ref, *refs):
    pieces, (out_ref, sems) = refs[: len(moves)], refs[-2:]
    copies = []
    for i, (flip, stride, first) in enumerate(moves):
        column = jnp.bitwise_xor(place_ref[0], flip) * stride + first
        there = out_ref.at[:, pl.ds(pl.multiple_of(column, span), pieces[i].shape[1])]
        copies.append(pltpu.make_async_copy(pieces[i], there, sems.at[i]))
        copies[-1].start()
    for copy in copies:
        copy.wait()


def prepare_kernel(count, rows, width, centres, obs_len, place_ref, *refs):
    pieces, (ydt_ref, solved_ref, ysum_ref) = refs[:count], refs[count:]
    offset = pl.multiple_of((place_ref[0] & 1) * (centres * obs_len), obs_len)
    window = pl.ds(offset, width)
    members = count * rows
    total = jnp.zeros((1, width), jnp.float32)
    for piece in pieces:
        total = total + jnp.sum(piece[0, :, window].astype(jnp.float32), axis=0, keepdims=True)
    centre = total / members
    for i, piece in enumerate(pieces):
        place = slice(i * rows, (i + 1) * rows)
        dev = piece[0, :, window].astype(jnp.float32) - centre
        ydt_ref[:width, place] = jnp.transpose(dev.astype(jnp.bfloat16))
        solved_ref[place, :] = piece[1, :, window]
    ydt_ref[width:, :] = jnp.ones((ydt_ref.shape[0] - width, members), jnp.bfloat16)
    ysum_ref[...] = jnp.dot(
        ydt_ref[:width, :],
        jnp.ones((members, ysum_ref.shape[1]), jnp.bfloat16),
        preferred_element_type=jnp.float32,
    )


def analyse_kernel(count, rows, span, obs_len, start, geometry, place_ref, block_ref, taper_ref, *refs):
    priors, (ydt_ref, solved_ref, ysum_ref, loc_ref) = refs[:count], refs[count : count + 4]
    outs, (var_ref, weight_ref) = refs[count + 4 : 2 * count + 4], refs[2 * count + 4 :]
    step = pl.program_id(0)
    per_worker, centres, band_blocks = geometry
    first_patch = place_ref[0] * per_worker + start
    first_block = place_ref[1] * band_blocks + place_ref[0] * centres - RIM_BLOCKS
    width = solved_ref.shape[1]
    members = count * rows
    patches = priors[0].shape[1] // span
    weight_ref[...] = jnp.zeros_like(weight_ref)
    for j in range(patches):
        patch = first_patch + step * patches + j
        for k in range(block_ref.shape[0]):
            row = pl.multiple_of((block_ref[k, patch] - first_block) * obs_len, obs_len)
            there = (pl.ds(row, obs_len), slice(j * span, (j + 1) * span))
            weight_ref[there] = weight_ref[there] + loc_ref[taper_ref[k, patch]]
    prior = jnp.concatenate([ref[...] for ref in priors], axis=0)
    product = jnp.dot(ydt_ref[...], prior, preferred_element_type=jnp.float32)
    mean = product[width : width + 1, :] * (1.0 / members)
    ysum = jnp.concatenate([ysum_ref[...]] * patches, axis=1)
    cov = product[:width, :] - ysum * mean
    tapered = (cov * weight_ref[...]).astype(jnp.bfloat16)
    increment = jnp.dot(solved_ref[...], tapered, preferred_element_type=jnp.float32)
    updated = (prior.astype(jnp.float32) + increment).astype(jnp.bfloat16)
    for i, out in enumerate(outs):
        out[...] = updated[i * rows : (i + 1) * rows, :]
    updated = updated.astype(jnp.float32)
    centre = jnp.sum(updated, axis=0, keepdims=True) * (1.0 / members)
    variance = jnp.sum((updated - centre) ** 2, axis=0, keepdims=True) * (1.0 / members)
    for j in range(patches):
        var_ref[pl.ds(step * patches + j, 1), :] = variance[:, j * span : (j + 1) * span]


def select_kernel(per_worker, owner_ref, place_ref, out_ref):
    me = place_ref[0]
    out_ref[...] = jnp.zeros_like(out_ref)
    lanes = lax.broadcasted_iota(jnp.int32, (1, out_ref.shape[1]), 1)

    def one(patch, filled):
        mine = owner_ref[patch] == me

        @pl.when(mine)
        def _():
            source = jnp.bitwise_xor(patch // per_worker, me) * per_worker + patch % per_worker
            out_ref[pl.ds(filled, 1), :] = (lanes == source).astype(jnp.float32)

        return filled + mine.astype(jnp.int32)

    lax.fori_loop(0, owner_ref.shape[0], one, jnp.int32(0))


def spread_kernel(select_ref, var_ref, out_ref):
    out_ref[...] = jnp.dot(
        select_ref[...],
        var_ref[...],
        precision=lax.Precision.HIGHEST,
        preferred_element_type=jnp.float32,
    )


def whole(shape):
    return pl.BlockSpec(shape, lambda *_: (0,) * len(shape))


def per_device(
    prior_ensemble,
    perturbed_measurements,
    solved_residuals,
    localisation_matrix,
    piece_owner_device,
    measurement_group_matrix,
    localisation_factors,
):
    rows, vector_span = prior_ensemble.shape
    taper_count, span, obs_len = localisation_matrix.shape
    count, bands = lax.axis_size("mem"), lax.axis_size("band")
    members = rows * count
    strip = vector_span // span
    band_blocks = perturbed_measurements.shape[1] // obs_len
    per_worker = strip // count
    centres = per_worker * band_blocks // strip
    assert centres * strip == per_worker * band_blocks and count & (count - 1) == 0
    window = 2 * RIM_BLOCKS + centres
    width = window * obs_len
    strip_position = lax.axis_index("band")
    me = lax.axis_index("mem")

    place = jnp.stack([me, strip_position]).astype(jnp.int32)
    sent = []

    def after_sent(x):
        if len(sent) >= IN_FLIGHT:
            x, sent[-IN_FLIGHT] = lax.optimization_barrier((x, sent[-IN_FLIGHT]))
        return x

    def partner(x, flip, after=()):
        if after:
            x = lax.optimization_barrier((x, *after))[0]
        pairs = [(i, i ^ flip) for i in range(count)]
        if flip == 1:
            return lax.ppermute(x, "mem", pairs)
        sent.append(lax.ppermute(after_sent(x), "mem", pairs))
        return sent[-1]

    pair_width = (window + centres) * obs_len

    chunk_patches = per_worker // CHUNKS
    chunk_span = chunk_patches * span

    select = pl.pallas_call(
        functools.partial(select_kernel, per_worker),
        grid_spec=pltpu.PrefetchScalarGridSpec(
            num_scalar_prefetch=2,
            grid=(1,),
            in_specs=[],
            out_specs=whole((2 * per_worker, strip)),
        ),
        out_shape=jax.ShapeDtypeStruct((2 * per_worker, strip), jnp.float32),
    )(piece_owner_device, place)
    taper = pl.pallas_call(
        functools.partial(taper_kernel, 1.0 / (members - 1)),
        out_shape=jax.ShapeDtypeStruct((taper_count, obs_len, span), jnp.float32),
        compiler_params=pltpu.CompilerParams(vmem_limit_bytes=VMEM_BYTES),
    )(localisation_matrix)

    order = list(range(2, count, 2)) + list(range(3, count, 2)) + [1]

    def outgoing(source, flip, chunk):
        first = (me ^ flip) * (per_worker * span) + chunk * chunk_span
        return lax.dynamic_slice_in_dim(source, first, chunk_span, 1)

    source, cut = prior_ensemble, []
    got = [{} for _ in range(CHUNKS)]
    for flip in order[:FIRST]:
        cut.append(outgoing(source, flip, 0))
        source, cut[-1] = lax.optimization_barrier((source, cut[-1]))
        got[0][flip] = partner(cut[-1], flip)
    both = jnp.stack([perturbed_measurements, solved_residuals])
    both, got[0][order[0]] = lax.optimization_barrier((both, got[0][order[0]]))
    up = [(i, i + 1) for i in range(bands - 1)]
    down = [(j, i) for i, j in up]
    rim = RIM_BLOCKS * obs_len
    before = lax.ppermute(both[:, :, -rim:], "band", up)
    after = lax.ppermute(both[:, :, :rim], "band", down)
    padded = jnp.concatenate([before, both, after], axis=2)

    def pair_window(flip):
        first = ((me ^ flip) >> 1) * (2 * centres * obs_len)
        return lax.dynamic_slice_in_dim(padded, first, pair_width, 2)

    for flip in order[FIRST:]:
        got[0][flip] = partner(outgoing(source, flip, 0), flip)
    even = {0: pair_window(0)}
    for flip in range(2, count, 2):
        even[flip] = partner(pair_window(flip), flip)
    for flip in order[:EARLY]:
        got[1][flip] = partner(outgoing(source, flip, 1), flip)
    even[0], select, taper = lax.optimization_barrier((even[0], select, taper))
    pieces = []
    for flip in range(0, count, 2):
        pieces += [even[flip], partner(even[flip], 1)]
    for chunk in range(1, CHUNKS):
        for flip in order:
            if flip not in got[chunk]:
                after = [pieces[flip - 2]] if chunk == 1 and flip & 1 and 1 < flip < count - 1 else []
                got[chunk][flip] = partner(outgoing(source, flip, chunk), flip, after)
    priors = [[pieces_of[i] for i in range(1, count)] for pieces_of in got]

    ydt, solved, ysum = pl.pallas_call(
        functools.partial(prepare_kernel, count, rows, width, centres, obs_len),
        grid_spec=pltpu.PrefetchScalarGridSpec(
            num_scalar_prefetch=1,
            grid=(1,),
            in_specs=[whole((2, rows, pair_width))] * count,
            out_specs=[
                whole((width + PAD_ROWS, members)),
                whole((members, width)),
                whole((width, span)),
            ],
        ),
        out_shape=[
            jax.ShapeDtypeStruct((width + PAD_ROWS, members), jnp.bfloat16),
            jax.ShapeDtypeStruct((members, width), jnp.bfloat16),
            jax.ShapeDtypeStruct((width, span), jnp.float32),
        ],
        compiler_params=pltpu.CompilerParams(vmem_limit_bytes=VMEM_BYTES),
    )(place, *pieces)

    step_span = STEP_PATCHES * span
    piece_spec = pl.BlockSpec((rows, step_span), lambda i, *_: (0, i))
    blocks, tapers = measurement_group_matrix.T, localisation_factors.T

    def analyse(chunk, prior):
        steps = chunk_patches // STEP_PATCHES

        def own(i, place_ref, *_):
            return 0, (place_ref[0] * CHUNKS + chunk) * steps + i

        *out, variance = pl.pallas_call(
            functools.partial(
                analyse_kernel,
                count,
                rows,
                span,
                obs_len,
                chunk * chunk_patches,
                (per_worker, centres, band_blocks),
            ),
            grid_spec=pltpu.PrefetchScalarGridSpec(
                num_scalar_prefetch=3,
                grid=(steps,),
                in_specs=[pl.BlockSpec((rows, step_span), own)]
                + [piece_spec] * (count - 1)
                + [
                    whole((width + PAD_ROWS, members)),
                    whole((members, width)),
                    whole((width, span)),
                    whole((taper_count, obs_len, span)),
                ],
                out_specs=[piece_spec] * count + [whole((chunk_patches, span))],
                scratch_shapes=[pltpu.VMEM((width, step_span), jnp.float32)],
            ),
            out_shape=[jax.ShapeDtypeStruct((rows, chunk_span), jnp.bfloat16)] * count
            + [jax.ShapeDtypeStruct((chunk_patches, span), jnp.float32)],
            compiler_params=pltpu.CompilerParams(vmem_limit_bytes=VMEM_BYTES),
        )(place, blocks, tapers, prior_ensemble, *prior, ydt, solved, ysum, taper)
        return out, variance

    def assemble(analysis, pieces, moves):
        base = [] if analysis is None else [analysis]
        return pl.pallas_call(
            functools.partial(assemble_kernel, moves, span),
            grid_spec=pltpu.PrefetchScalarGridSpec(
                num_scalar_prefetch=1,
                grid=(1,),
                in_specs=[whole((rows, chunk_span))] * len(pieces)
                + [pl.BlockSpec(memory_space=pl.ANY)] * len(base),
                out_specs=pl.BlockSpec(memory_space=pl.ANY),
                scratch_shapes=[pltpu.SemaphoreType.DMA((len(pieces),))],
            ),
            out_shape=jax.ShapeDtypeStruct(prior_ensemble.shape, prior_ensemble.dtype),
            input_output_aliases={1 + len(pieces): 0} if base else {},
            compiler_params=pltpu.CompilerParams(vmem_limit_bytes=ASSEMBLE_BYTES if base else VMEM_BYTES),
        )(place, *pieces, *base)

    analysis = None
    gathered, spread_flip = [], 1
    back = order
    for chunk in range(CHUNKS):
        out, variance = analyse(chunk, priors[chunk])
        gathered.append(variance)
        final = chunk == CHUNKS - 1
        arrived, moves = [], []
        for i, flip in enumerate([0] + back):
            if final and spread_flip < count:
                if spread_flip == 1:
                    gathered = jnp.concatenate(gathered, axis=0)
                gathered = jnp.concatenate([gathered, partner(gathered, spread_flip)], axis=0)
                spread_flip *= 2
            if final and i == ASSEMBLE_BEFORE:
                out[flip], analysis = lax.optimization_barrier((out[flip], analysis))
            arrived.append(partner(out[flip], flip) if flip else out[0])
            moves.append((flip, per_worker * span, chunk * chunk_span))
            if len(moves) == count or (final and len(moves) == count // 2 + 1):
                analysis = assemble(analysis, arrived, tuple(moves))
                arrived, moves = [], []
        if moves:
            analysis = assemble(analysis, arrived, tuple(moves))
    assert spread_flip == count
    spread = pl.pallas_call(
        spread_kernel,
        out_shape=jax.ShapeDtypeStruct((2 * per_worker, span), jnp.float32),
    )(select, gathered)
    return analysis, spread


def solution(mesh):
    return jax.shard_map(
        per_device,
        mesh=mesh,
        in_specs=(
            P("mem", "band"),
            P("mem", "band"),
            P("mem", "band"),
            P(),
            P("band"),
            P("band", None),
            P("band", None),
        ),
        out_specs=(P("mem", "band"), P(("band", "mem"), None)),
        check_vma=False,
    )
```
